32 devices in a mesh: col: 4 (over z), row: 8 (over y, x, core).
Axes of the slice: x: 2, y: 2, z: 4, core: 2. Of those that a mesh axis runs over, the one named last changes fastest.
Arguments:
- factor: float32 [8192, 2048], P('row', 'col'), may hold values from -100 to 100
- support: int32 [16, 64], P(None, 'row'), may hold values from 0 to 1, as said below
- plan: int32 [2, 16], replicated, may hold values from 0 to 15, as said below
Outputs:
- rotated_factor: float32 [8192, 2048], P('row', 'col')
The draws below stay inside these ranges and needn't reach their ends.
Inputs may be any that keep to these rules, and one draw needn't show every extreme that they name: Every column block has at least one row block in its support. `plan`: each row is a permutation; cut each round's row into groups of 4 consecutive positions (group g on index g of col); the 4 blocks of any group sit in 4 different groups of the previous round's row, where the order before round 0 is 0, 1, ..., 15.
All inputs are finite; a program needn't handle non-finite values.
Results may differ from the reference program's by a relative error of at most 0.0003.
Values sent between devices are 32-bit elements; how exact they have to be, the bound alone decides.
A program may use at most 128 MiB of HBM per device.

```python
import math
import jax
import jax.numpy as jnp
from jax import lax

W = 128
NCB = 16
RB = 128
ROUNDS = 2
NB = 64
ROWS = 8192
COLS = 2048
N_COL = 4


def draw_factor(key, part):
    keys = jax.random.split(key, 5)
    row_scale = jnp.exp(jax.random.uniform(keys[0], (ROWS, 1), jnp.float32, math.log(0.3), math.log(3.0)))
    col_scale = jnp.exp(jax.random.uniform(keys[1], (1, COLS), jnp.float32, math.log(0.3), math.log(3.0)))
    loading = jax.random.uniform(keys[2], (1, COLS), jnp.float32, -1.5, 1.5)
    common = jnp.clip(jax.random.normal(keys[3], (ROWS, 1), jnp.float32), -4.0, 4.0)
    noise = jnp.clip(jax.random.normal(keys[4], (ROWS, COLS), jnp.float32), -4.0, 4.0)
    return (row_scale * col_scale * (common * loading + noise)).astype(jnp.float32)


def draw_support(key, part):
    vote_key, anchor_key = jax.random.split(key)
    block_ids = jnp.arange(NB, dtype=jnp.int32)
    threshold = 25 + 70 * block_ids // NB
    votes = jax.random.randint(vote_key, (NCB, NB), 0, 100)
    anchors = jax.random.randint(anchor_key, (NCB, 1), 0, NB)
    chosen = jnp.logical_or(votes < threshold[None, :], block_ids[None, :] == anchors)
    return jnp.where(chosen, 1, 0).astype(jnp.int32)


def draw_plan(key, part):
    group_count = N_COL
    previous = jnp.arange(NCB, dtype=jnp.int32)
    rounds_list = []

    def shuffled(one_key):
        return jax.random.permutation(one_key, group_count)
    for round_index in range(ROUNDS):
        round_key = jax.random.fold_in(key, round_index)
        shift_key, order_key = jax.random.split(round_key)
        offsets = jax.random.permutation(shift_key, group_count)
        inner = jax.vmap(shuffled)(jax.random.split(order_key, group_count))
        targets = jnp.broadcast_to(jnp.arange(group_count)[:, None], (group_count, group_count))
        slot_ids = jnp.broadcast_to(jnp.arange(group_count)[None, :], (group_count, group_count))
        sources = (targets + offsets[slot_ids]) % group_count
        local_ids = inner[sources, targets]
        previous = previous[(sources * group_count + local_ids).reshape(NCB)]
        rounds_list.append(previous)
    return jnp.stack(rounds_list).astype(jnp.int32)


def setup_inputs(seed: int = 0) -> dict:
    seeds = jax.random.split(jax.random.key(seed), 4)
    factor = draw_factor(jax.random.fold_in(seeds[3], 71), 0)
    support = draw_support(jax.random.fold_in(seeds[3], 71), 0)
    plan = draw_plan(jax.random.fold_in(seeds[3], 71), 0)
    return dict(factor=factor, support=support, plan=plan)


precise = lax.Precision.HIGHEST
damping = 0.01

def skew_terms(gram_rows, diag_rows, diag_cols):
    spread = diag_rows[:, :, None] - diag_cols[:, None, :]
    joined = diag_rows[:, :, None] + diag_cols[:, None, :]
    return gram_rows * spread / (spread * spread + gram_rows * gram_rows + damping * joined * joined)

def cayley(skew_matrix):
    size_here = skew_matrix.shape[0]
    identity = jnp.eye(size_here, dtype=jnp.float32)
    halved = 0.5 * skew_matrix
    minus_half = identity - halved
    numerator = jnp.dot(minus_half, minus_half, precision=precise)
    definite = identity + jnp.dot(halved.T, halved, precision=precise)
    lower_factor = jnp.linalg.cholesky(definite)
    return jax.scipy.linalg.cho_solve((lower_factor, True), numerator)

def reference(factor, support, plan):
    total_rows = factor.shape[0]
    row_mask = jnp.repeat(support.T, RB, axis=0).astype(jnp.float32)
    current = factor.reshape(total_rows, NCB, W) * row_mask[:, :, None]
    previous = jnp.arange(NCB, dtype=jnp.int32)
    for round_index in range(ROUNDS):
        order_now = plan[round_index]
        located = jnp.argsort(previous)[order_now]
        arranged = current[:, located, :]
        paired = arranged.reshape(total_rows, NCB // 2, 2 * W)
        gram_matrix = jnp.einsum('rpi,rpj->pij', paired, paired, precision=precise)
        diagonal_terms = jnp.diagonal(gram_matrix, axis1=1, axis2=2)
        skew_matrix = skew_terms(gram_matrix, diagonal_terms, diagonal_terms)
        rotations = jax.vmap(cayley)(skew_matrix)
        rotated = jnp.einsum('rpi,pij->rpj', paired, rotations, precision=precise)
        current = rotated.reshape(total_rows, NCB, W)
        previous = order_now
    return current.reshape(total_rows, NCB * W)
```

```python
import functools

import jax
import jax.numpy as jnp
from jax import lax
from jax.experimental import pallas as pl
from jax.experimental.pallas import tpu as pltpu
from jax.sharding import PartitionSpec as P

W = 128
RB = 128
ROUNDS = 2
CHUNKS = 4
SCALED_STEPS = 7
TRUE_STEPS = 2
DAMPING = 0.01
F32 = jnp.float32
BF16 = jnp.bfloat16
MESH = pl.DeviceIdType.MESH


def split(x):
    high = x.astype(BF16)
    return high, (x - high.astype(F32)).astype(BF16)


def dot(a, b):
    return jnp.dot(a, b, preferred_element_type=F32)


def dot3(a, b):
    a_high, a_low = split(a)
    b_high, b_low = split(b)
    return dot(a_high, b_high) + (dot(a_high, b_low) + dot(a_low, b_high))


def dot_t(a, b):
    return lax.dot_general(a, b, (((0,), (0,)), ((), ())), preferred_element_type=F32)


def rotation(gram, eye, stack):
    size = gram.shape[0]
    on_diagonal = gram * eye
    diag_rows = jnp.sum(on_diagonal, axis=1, keepdims=True)
    diag_cols = jnp.sum(on_diagonal, axis=0, keepdims=True)
    spread = diag_rows - diag_cols
    joined = diag_rows + diag_cols
    half = 0.5 * gram * spread / (spread * spread + gram * gram + DAMPING * joined * joined)
    squared = dot3(half, half)
    total = jnp.sum(jnp.sum(squared * squared, axis=1, keepdims=True), axis=0, keepdims=True)
    upper = 1.0 + 1.001 * jnp.sqrt(0.5 * total)
    stack[:size] = eye - squared
    stack[size:] = eye - half

    def scaled(_, bounds):
        low, high = bounds
        scale = 2.0 / (low + high)
        delta = (high - low) / (high + low)
        factor = (2.0 * scale) * eye - (scale * scale) * stack[:size]
        stack[...] = dot3(stack[...], factor)
        return 1.0 - delta * delta, jnp.ones_like(high)

    lax.fori_loop(0, SCALED_STEPS, scaled, (jnp.ones_like(upper), upper))

    def true(_, carry):
        inverse = stack[size:]
        residual = (eye - inverse) - dot3(half, inverse)
        stack[size:] = inverse + dot3(inverse, residual)
        return carry

    lax.fori_loop(0, TRUE_STEPS, true, 0)
    return 2.0 * stack[size:] - eye


def kernel(
    groups, members, factor_ref, support_ref, plan_ref, out_ref,
    cur, send, recv, gram, gram_in, rot, rot_pair, stack,
    move_send, move_recv, swap_send, swap_recv, sum_send, sum_recv, rot_send, rot_recv,
):
    slots, rows, _ = cur.shape
    size = 2 * W
    chunk = rows // CHUNKS
    chips = members // 2
    stages = chips.bit_length() - 1
    g = lax.axis_index("col")
    m = lax.axis_index("row")
    core = lax.rem(m, 2)
    chip = m // 2
    partner = m + 1 - 2 * core

    def flipped(bit):
        step = 1 << bit
        on = lax.rem(chip // step, 2)
        return (chip + step - 2 * step * on) * 2 + core

    peers = [{"col": lax.rem(g + o, groups), "row": m} for o in range(1, groups)]
    peers += [{"col": g, "row": partner}]
    peers += [{"col": g, "row": flipped(b)} for b in range(stages)]
    barrier = pltpu.get_barrier_semaphore()
    for peer in peers:
        pl.semaphore_signal(barrier, inc=1, device_id=peer, device_id_type=MESH)

    row_ids = lax.broadcasted_iota(jnp.int32, (size, size), 0)
    col_ids = lax.broadcasted_iota(jnp.int32, (size, size), 1)
    eye = (row_ids == col_ids).astype(F32)

    for s in range(slots):
        for b in range(rows // RB):
            span = pl.ds(b * RB, RB)
            weight = support_ref[g * slots + s, b].astype(F32)
            cur[s, span] = factor_ref[span, s * W:(s + 1) * W] * weight

    def before(r, position):
        return position if r == 0 else plan_ref[r - 1, position]

    blocks = groups * slots
    pick, take = [], []
    for r in range(ROUNDS):
        dest = []
        for s in range(slots):
            block = before(r, g * slots + s)
            dest.append(sum(
                jnp.where(plan_ref[r, j] == block, j // slots, 0) for j in range(blocks)))
        pick.append([
            jnp.minimum(slots - 1, sum(
                jnp.where(dest[s] == lax.rem(g + o, groups), s, 0) for s in range(slots)))
            for o in range(groups)])
        take.append([])
        for s in range(slots):
            block = plan_ref[r, g * slots + s]
            take[r].append(jnp.minimum(groups - 1, sum(
                jnp.where(before(r, j) == block, j // slots, 0) for j in range(blocks))))

    pl.semaphore_wait(barrier, len(peers))

    copies = []

    def start(copy):
        copy.start()
        copies.append(copy)
        return copy

    def dispatch(r, q):
        span = pl.ds(q * chunk, chunk)
        out = []
        for o in range(1, groups):
            send[r, o - 1, span] = cur[pick[r][o], span]
            out.append(start(pltpu.make_async_remote_copy(
                src_ref=send.at[r, o - 1, span],
                dst_ref=recv[r][q].at[g],
                send_sem=move_send.at[r, q, o - 1],
                recv_sem=move_recv.at[r, q, o - 1],
                device_id=peers[o - 1],
                device_id_type=MESH,
            )))
        recv[r][q][g] = cur[pick[r][0], span]
        return out

    def load_pair(r, k, q):
        held = recv[r][q]
        return jnp.concatenate([held[take[r][2 * k]], held[take[r][2 * k + 1]]], axis=1)

    moves = [dispatch(0, q) for q in range(CHUNKS)]
    for r in range(ROUNDS):
        for q in range(CHUNKS):
            for copy in moves[q]:
                copy.wait_recv()
            for k in range(2):
                high, low = split(load_pair(r, k, q))
                mixed = dot_t(high, low)
                part = dot_t(high, high) + (mixed + mixed.T)
                gram_in[r, k] = part if q == 0 else gram_in[r, k] + part
        swap = start(pltpu.make_async_remote_copy(
            src_ref=gram_in.at[r, 1 - core],
            dst_ref=gram_in.at[r, 2],
            send_sem=swap_send.at[r],
            recv_sem=swap_recv.at[r],
            device_id=peers[groups - 1],
            device_id_type=MESH,
        ))
        swap.wait_recv()
        total = gram_in[r, core] + gram_in[r, 2]
        for stage in range(stages):
            gram[r, 2 * stage] = total
            pair = []
            for h in range(2):
                bit = (stage + h * (stages // 2)) % stages
                part = pl.ds(h * W, W)
                pair.append(start(pltpu.make_async_remote_copy(
                    src_ref=gram.at[r, 2 * stage, part],
                    dst_ref=gram.at[r, 2 * stage + 1, part],
                    send_sem=sum_send.at[r, stage, h],
                    recv_sem=sum_recv.at[r, stage, h],
                    device_id=peers[groups + bit],
                    device_id_type=MESH,
                )))
            for copy in pair:
                copy.wait_recv()
            total = total + gram[r, 2 * stage + 1]
        rot[r, 0] = rotation(total, eye, stack)
        back = start(pltpu.make_async_remote_copy(
            src_ref=rot.at[r, 0],
            dst_ref=rot.at[r, 1],
            send_sem=rot_send.at[r],
            recv_sem=rot_recv.at[r],
            device_id=peers[groups - 1],
            device_id_type=MESH,
        ))
        back.wait_recv()
        rot_pair[core] = rot[r, 0]
        rot_pair[1 - core] = rot[r, 1]
        moves = []
        for q in range(CHUNKS):
            span = pl.ds(q * chunk, chunk)
            for k in range(2):
                turned = dot3(load_pair(r, k, q), rot_pair[k])
                if r == ROUNDS - 1:
                    out_ref[span, k * size:(k + 1) * size] = turned
                else:
                    cur[2 * k, span] = turned[:, :W]
                    cur[2 * k + 1, span] = turned[:, W:]
            if r < ROUNDS - 1:
                moves.append(dispatch(r + 1, q))
    for copy in copies:
        copy.wait_send()


def on_device(groups, members, factor, support, plan):
    rows = factor.shape[0]
    slots = factor.shape[1] // W
    chips = members // 2
    stages = chips.bit_length() - 1
    assert slots == 4 and chips == 1 << stages and stages >= 1
    size = 2 * W
    dma = pltpu.SemaphoreType.DMA
    vmem = pl.BlockSpec(memory_space=pltpu.VMEM)
    smem = pl.BlockSpec(memory_space=pltpu.SMEM)
    return pl.pallas_call(
        functools.partial(kernel, groups, members),
        out_shape=jax.ShapeDtypeStruct(factor.shape, F32),
        in_specs=[vmem, smem, smem],
        out_specs=vmem,
        scratch_shapes=[
            pltpu.VMEM((slots, rows, W), F32),
            pltpu.VMEM((ROUNDS, groups - 1, rows, W), F32),
            [[pltpu.VMEM((groups, rows // CHUNKS, W), F32)] * CHUNKS] * ROUNDS,
            pltpu.VMEM((ROUNDS, 2 * stages, size, size), F32),
            pltpu.VMEM((ROUNDS, 3, size, size), F32),
            pltpu.VMEM((ROUNDS, 2, size, size), F32),
            pltpu.VMEM((2, size, size), F32),
            pltpu.VMEM((2 * size, size), F32),
            dma((ROUNDS, CHUNKS, groups - 1)),
            dma((ROUNDS, CHUNKS, groups - 1)),
            dma((ROUNDS,)),
            dma((ROUNDS,)),
            dma((ROUNDS, stages, 2)),
            dma((ROUNDS, stages, 2)),
            dma((ROUNDS,)),
            dma((ROUNDS,)),
        ],
        compiler_params=pltpu.CompilerParams(
            collective_id=0, has_side_effects=True, vmem_limit_bytes=48 * 1024 * 1024
        ),
    )(factor, support, plan)


def solution(mesh):
    return jax.shard_map(
        functools.partial(on_device, mesh.shape["col"], mesh.shape["row"]),
        mesh=mesh,
        in_specs=(P("row", "col"), P(None, "row"), P()),
        out_specs=P("row", "col"),
        check_vma=False,
    )
```

```python
import functools

import jax
import jax.numpy as jnp
from jax import lax
from jax.experimental import pallas as pl
from jax.experimental.pallas import tpu as pltpu
from jax.sharding import PartitionSpec as P

W = 128
RB = 128
ROUNDS = 2
CHUNKS = 4
SCALED_STEPS = 7
TRUE_STEPS = 2
DAMPING = 0.01
F32 = jnp.float32
BF16 = jnp.bfloat16
MESH = pl.DeviceIdType.MESH


def split(x):
    high = x.astype(BF16)
    return high, (x - high.astype(F32)).astype(BF16)


def dot(a, b):
    return jnp.dot(a, b, preferred_element_type=F32)


def dot3(a, b):
    a_high, a_low = split(a)
    b_high, b_low = split(b)
    return dot(a_high, b_high) + (dot(a_high, b_low) + dot(a_low, b_high))


def dot_t(a, b):
    return lax.dot_general(a, b, (((0,), (0,)), ((), ())), preferred_element_type=F32)


def rotation(gram, eye, stack):
    size = gram.shape[0]
    on_diagonal = gram * eye
    diag_rows = jnp.sum(on_diagonal, axis=1, keepdims=True)
    diag_cols = jnp.sum(on_diagonal, axis=0, keepdims=True)
    spread = diag_rows - diag_cols
    joined = diag_rows + diag_cols
    half = 0.5 * gram * spread / (spread * spread + gram * gram + DAMPING * joined * joined)
    squared = dot3(half, half)
    total = jnp.sum(jnp.sum(squared * squared, axis=1, keepdims=True), axis=0, keepdims=True)
    upper = 1.0 + 1.001 * jnp.sqrt(0.5 * total)
    stack[:size] = eye - squared
    stack[size:] = eye - half

    def scaled(_, bounds):
        low, high = bounds
        scale = 2.0 / (low + high)
        delta = (high - low) / (high + low)
        factor = (2.0 * scale) * eye - (scale * scale) * stack[:size]
        stack[...] = dot3(stack[...], factor)
        return 1.0 - delta * delta, jnp.ones_like(high)

    lax.fori_loop(0, SCALED_STEPS, scaled, (jnp.ones_like(upper), upper))

    def true(_, carry):
        inverse = stack[size:]
        residual = (eye - inverse) - dot3(half, inverse)
        stack[size:] = inverse + dot3(inverse, residual)
        return carry

    lax.fori_loop(0, TRUE_STEPS, true, 0)
    return 2.0 * stack[size:] - eye


def pack(gram):
    first, last = gram[:W, :W], gram[W:, W:]
    row_ids = lax.broadcasted_iota(jnp.int32, (W, W), 0)
    col_ids = lax.broadcasted_iota(jnp.int32, (W, W), 1)
    tile = jnp.where(row_ids >= col_ids, first, last)
    diagonal = jnp.sum(jnp.where(row_ids == col_ids, last, 0.0), axis=0, keepdims=True)
    return gram[:W, W:], tile, jnp.broadcast_to(diagonal, (8, W))


def unpack(packed):
    cross, tile, diagonal = packed[:W], packed[W:2 * W], packed[2 * W:2 * W + 1]
    row_ids = lax.broadcasted_iota(jnp.int32, (W, W), 0)
    col_ids = lax.broadcasted_iota(jnp.int32, (W, W), 1)
    lower = jnp.where(row_ids > col_ids, tile, 0.0)
    upper = jnp.where(row_ids < col_ids, tile, 0.0)
    first = lower + lower.T + jnp.where(row_ids == col_ids, tile, 0.0)
    last = upper + upper.T + jnp.where(row_ids == col_ids, diagonal, 0.0)
    top = jnp.concatenate([first, cross], axis=1)
    return jnp.concatenate([top, jnp.concatenate([cross.T, last], axis=1)], axis=0)


def kernel(
    groups, members, factor_ref, support_ref, plan_ref, out_ref,
    held, cur, send, recv, acc, gram, gram_in, rot, rot_pair, stack,
    load_sem, move_send, move_recv, swap_send, swap_recv, sum_send, sum_recv, rot_send, rot_recv,
):
    slots, rows, _ = cur.shape
    size = 2 * W
    chunk = rows // CHUNKS
    chips = members // 2
    stages = chips.bit_length() - 1
    g = lax.axis_index("col")
    m = lax.axis_index("row")
    core = lax.rem(m, 2)
    chip = m // 2
    partner = m + 1 - 2 * core

    def flipped(bit):
        step = 1 << bit
        on = lax.rem(chip // step, 2)
        return (chip + step - 2 * step * on) * 2 + core

    loads = []
    for q in range(CHUNKS):
        span = pl.ds(q * chunk, chunk)
        loads.append(pltpu.make_async_copy(factor_ref.at[span], held.at[span], load_sem.at[q]))
        loads[q].start()

    peers = [{"col": lax.rem(g + o, groups), "row": m} for o in range(1, groups)]
    peers += [{"col": g, "row": partner}]
    peers += [{"col": g, "row": flipped(b)} for b in range(stages)]
    barrier = pltpu.get_barrier_semaphore()
    for peer in peers:
        pl.semaphore_signal(barrier, inc=1, device_id=peer, device_id_type=MESH)

    row_ids = lax.broadcasted_iota(jnp.int32, (size, size), 0)
    col_ids = lax.broadcasted_iota(jnp.int32, (size, size), 1)
    eye = (row_ids == col_ids).astype(F32)

    def mask(q):
        loads[q].wait()
        for s in range(slots):
            for b in range(q * chunk // RB, (q + 1) * chunk // RB):
                span = pl.ds(b * RB, RB)
                weight = support_ref[b, g * slots + s].astype(F32)
                cur[s, span] = held[span, s * W:(s + 1) * W] * weight

    def before(r, position):
        return position if r == 0 else plan_ref[r - 1, position]

    blocks = groups * slots
    pick, take = [], []
    for r in range(ROUNDS):
        dest = []
        for s in range(slots):
            block = before(r, g * slots + s)
            dest.append(sum(
                jnp.where(plan_ref[r, j] == block, j // slots, 0) for j in range(blocks)))
        pick.append([
            jnp.minimum(slots - 1, sum(
                jnp.where(dest[s] == lax.rem(g + o, groups), s, 0) for s in range(slots)))
            for o in range(groups)])
        take.append([])
        for s in range(slots):
            block = plan_ref[r, g * slots + s]
            take[r].append(jnp.minimum(groups - 1, sum(
                jnp.where(before(r, j) == block, j // slots, 0) for j in range(blocks))))

    pl.semaphore_wait(barrier, len(peers))

    copies, stores = [], []

    def start(copy):
        copy.start()
        copies.append(copy)
        return copy

    def dispatch(r, q):
        span = pl.ds(q * chunk, chunk)
        out = []
        for o in range(1, groups):
            send[r, o - 1, span] = cur[pick[r][o], span]
            out.append(start(pltpu.make_async_remote_copy(
                src_ref=send.at[r, o - 1, span],
                dst_ref=recv[r][q].at[g],
                send_sem=move_send.at[r, q, o - 1],
                recv_sem=move_recv.at[r, q, o - 1],
                device_id=peers[o - 1],
                device_id_type=MESH,
            )))
        recv[r][q][g] = cur[pick[r][0], span]
        return out

    def load_pair(r, k, q):
        held = recv[r][q]
        return jnp.concatenate([held[take[r][2 * k]], held[take[r][2 * k + 1]]], axis=1)

    moves = []
    for q in range(CHUNKS):
        mask(q)
        moves.append(dispatch(0, q))
    for r in range(ROUNDS):
        for q in range(CHUNKS):
            for copy in moves[q]:
                copy.wait_recv()
            for k in range(2):
                high, low = split(load_pair(r, k, q))
                mixed = dot_t(high, low)
                part = dot_t(high, high) + (mixed + mixed.T)
                acc[k] = part if q == 0 else acc[k] + part
        for k in range(2):
            cross, tile, diagonal = pack(acc[k])
            gram_in[r, k, :W] = cross
            gram_in[r, k, W:size] = tile
            gram_in[r, k, size:] = diagonal
        swap = start(pltpu.make_async_remote_copy(
            src_ref=gram_in.at[r, 1 - core],
            dst_ref=gram_in.at[r, 2],
            send_sem=swap_send.at[r],
            recv_sem=swap_recv.at[r],
            device_id=peers[groups - 1],
            device_id_type=MESH,
        ))
        swap.wait_recv()
        total = gram_in[r, core] + gram_in[r, 2]
        for stage in range(stages):
            gram[r, 2 * stage] = total
            pair = []
            for h in range(2):
                bit = (stage + h * (stages // 2)) % stages
                part = pl.ds(0, W) if h == 0 else pl.ds(W, W + 8)
                pair.append(start(pltpu.make_async_remote_copy(
                    src_ref=gram.at[r, 2 * stage, part],
                    dst_ref=gram.at[r, 2 * stage + 1, part],
                    send_sem=sum_send.at[r, stage, h],
                    recv_sem=sum_recv.at[r, stage, h],
                    device_id=peers[groups + bit],
                    device_id_type=MESH,
                )))
            for copy in pair:
                copy.wait_recv()
            total = total + gram[r, 2 * stage + 1]
        rot[r, 0] = rotation(unpack(total), eye, stack)
        back = start(pltpu.make_async_remote_copy(
            src_ref=rot.at[r, 0],
            dst_ref=rot.at[r, 1],
            send_sem=rot_send.at[r],
            recv_sem=rot_recv.at[r],
            device_id=peers[groups - 1],
            device_id_type=MESH,
        ))
        back.wait_recv()
        rot_pair[core] = rot[r, 0]
        rot_pair[1 - core] = rot[r, 1]
        moves = []
        for q in range(CHUNKS):
            span = pl.ds(q * chunk, chunk)
            for k in range(2):
                turned = dot3(load_pair(r, k, q), rot_pair[k])
                if r == ROUNDS - 1:
                    held[span, k * size:(k + 1) * size] = turned
                else:
                    cur[2 * k, span] = turned[:, :W]
                    cur[2 * k + 1, span] = turned[:, W:]
            if r == ROUNDS - 1:
                stores.append(pltpu.make_async_copy(held.at[span], out_ref.at[span], load_sem.at[q]))
                stores[q].start()
            else:
                moves.append(dispatch(r + 1, q))
    for copy in copies:
        copy.wait_send()
    for copy in stores:
        copy.wait()


def on_device(groups, members, factor, support, plan):
    rows = factor.shape[0]
    slots = factor.shape[1] // W
    chips = members // 2
    stages = chips.bit_length() - 1
    assert slots == 4 and chips == 1 << stages and stages >= 1
    size = 2 * W
    dma = pltpu.SemaphoreType.DMA
    smem = pl.BlockSpec(memory_space=pltpu.SMEM)
    return pl.pallas_call(
        functools.partial(kernel, groups, members),
        out_shape=jax.ShapeDtypeStruct(factor.shape, F32),
        in_specs=[pl.BlockSpec(memory_space=pl.ANY), smem, smem],
        out_specs=pl.BlockSpec(memory_space=pl.ANY),
        scratch_shapes=[
            pltpu.VMEM(factor.shape, F32),
            pltpu.VMEM((slots, rows, W), F32),
            pltpu.VMEM((ROUNDS, groups - 1, rows, W), F32),
            [[pltpu.VMEM((groups, rows // CHUNKS, W), F32)] * CHUNKS] * ROUNDS,
            pltpu.VMEM((2, size, size), F32),
            pltpu.VMEM((ROUNDS, 2 * stages, size + 8, W), F32),
            pltpu.VMEM((ROUNDS, 3, size + 8, W), F32),
            pltpu.VMEM((ROUNDS, 2, size, size), F32),
            pltpu.VMEM((2, size, size), F32),
            pltpu.VMEM((2 * size, size), F32),
            dma((CHUNKS,)),
            dma((ROUNDS, CHUNKS, groups - 1)),
            dma((ROUNDS, CHUNKS, groups - 1)),
            dma((ROUNDS,)),
            dma((ROUNDS,)),
            dma((ROUNDS, stages, 2)),
            dma((ROUNDS, stages, 2)),
            dma((ROUNDS,)),
            dma((ROUNDS,)),
        ],
        compiler_params=pltpu.CompilerParams(
            collective_id=0, has_side_effects=True, vmem_limit_bytes=123 * 512 * 1024
        ),
    )(factor, support.T, plan)


def solution(mesh):
    return jax.shard_map(
        functools.partial(on_device, mesh.shape["col"], mesh.shape["row"]),
        mesh=mesh,
        in_specs=(P("row", "col"), P(None, "row"), P()),
        out_specs=P("row", "col"),
        check_vma=False,
    )
```

```python
import functools

import jax
import jax.numpy as jnp
from jax import lax
from jax.experimental import pallas as pl
from jax.experimental.pallas import tpu as pltpu
from jax.sharding import PartitionSpec as P

W = 128
RB = 128
ROUNDS = 2
CHUNKS = 4
SCALED_STEPS = 7
TRUE_STEPS = 2
DAMPING = 0.01
F32 = jnp.float32
BF16 = jnp.bfloat16
MESH = pl.DeviceIdType.MESH


def split(x):
    high = x.astype(BF16)
    return high, (x - high.astype(F32)).astype(BF16)


def dot(a, b):
    return jnp.dot(a, b, preferred_element_type=F32)


def dot3(a, b):
    a_high, a_low = split(a)
    b_high, b_low = split(b)
    return dot(a_high, b_high) + (dot(a_high, b_low) + dot(a_low, b_high))


def dot_t(a, b):
    return lax.dot_general(a, b, (((0,), (0,)), ((), ())), preferred_element_type=F32)


def rotation(gram, eye, stack):
    size = gram.shape[0]
    on_diagonal = gram * eye
    diag_rows = jnp.sum(on_diagonal, axis=1, keepdims=True)
    diag_cols = jnp.sum(on_diagonal, axis=0, keepdims=True)
    spread = diag_rows - diag_cols
    joined = diag_rows + diag_cols
    half = 0.5 * gram * spread / (spread * spread + gram * gram + DAMPING * joined * joined)
    squared = dot3(half, half)
    total = jnp.sum(jnp.sum(squared * squared, axis=1, keepdims=True), axis=0, keepdims=True)
    upper = 1.0 + 1.001 * jnp.sqrt(0.5 * total)
    stack[:size] = eye - squared
    stack[size:] = eye - half

    def scaled(_, bounds):
        low, high = bounds
        scale = 2.0 / (low + high)
        delta = (high - low) / (high + low)
        factor = (2.0 * scale) * eye - (scale * scale) * stack[:size]
        stack[...] = dot3(stack[...], factor)
        return 1.0 - delta * delta, jnp.ones_like(high)

    lax.fori_loop(0, SCALED_STEPS, scaled, (jnp.ones_like(upper), upper))

    def true(_, carry):
        inverse = stack[size:]
        residual = (eye - inverse) - dot3(half, inverse)
        stack[size:] = inverse + dot3(inverse, residual)
        return carry

    lax.fori_loop(0, TRUE_STEPS, true, 0)
    return 2.0 * stack[size:] - eye


def pack(gram):
    first, last = gram[:W, :W], gram[W:, W:]
    row_ids = lax.broadcasted_iota(jnp.int32, (W, W), 0)
    col_ids = lax.broadcasted_iota(jnp.int32, (W, W), 1)
    tile = jnp.where(row_ids >= col_ids, first, last)
    diagonal = jnp.sum(jnp.where(row_ids == col_ids, last, 0.0), axis=0, keepdims=True)
    return gram[:W, W:], tile, jnp.broadcast_to(diagonal, (8, W))


def unpack(packed):
    cross, tile, diagonal = packed[:W], packed[W:2 * W], packed[2 * W:2 * W + 1]
    row_ids = lax.broadcasted_iota(jnp.int32, (W, W), 0)
    col_ids = lax.broadcasted_iota(jnp.int32, (W, W), 1)
    lower = jnp.where(row_ids > col_ids, tile, 0.0)
    upper = jnp.where(row_ids < col_ids, tile, 0.0)
    first = lower + lower.T + jnp.where(row_ids == col_ids, tile, 0.0)
    last = upper + upper.T + jnp.where(row_ids == col_ids, diagonal, 0.0)
    top = jnp.concatenate([first, cross], axis=1)
    return jnp.concatenate([top, jnp.concatenate([cross.T, last], axis=1)], axis=0)


def kernel(
    groups, members, factor_ref, support_ref, plan_ref, out_ref,
    held, cur, send, recv, early_out, early_in, turn_out, turns,
    acc, gram, gram_in, rot, rot_pair, stack,
    load_sem, move_send, move_recv, early_send, early_recv, turn_send, turn_recv, spread_send, spread_recv,
    swap_send, swap_recv, sum_send, sum_recv, rot_send, rot_recv,
):
    slots, rows, _ = cur.shape
    size = 2 * W
    chunk = rows // CHUNKS
    chips = members // 2
    stages = chips.bit_length() - 1
    g = lax.axis_index("col")
    m = lax.axis_index("row")
    core = lax.rem(m, 2)
    chip = m // 2
    partner = m + 1 - 2 * core

    def flipped(bit):
        step = 1 << bit
        on = lax.rem(chip // step, 2)
        return (chip + step - 2 * step * on) * 2 + core

    loads = []
    for q in range(CHUNKS):
        span = pl.ds(q * chunk, chunk)
        loads.append(pltpu.make_async_copy(factor_ref.at[span], held.at[span], load_sem.at[q]))
        loads[q].start()

    peers = [{"col": lax.rem(g + o, groups), "row": m} for o in range(1, groups)]
    peers += [{"col": g, "row": partner}]
    peers += [{"col": g, "row": flipped(b)} for b in range(stages)]
    barrier = pltpu.get_barrier_semaphore()
    for peer in peers:
        pl.semaphore_signal(barrier, inc=1, device_id=peer, device_id_type=MESH)

    row_ids = lax.broadcasted_iota(jnp.int32, (size, size), 0)
    col_ids = lax.broadcasted_iota(jnp.int32, (size, size), 1)
    eye = (row_ids == col_ids).astype(F32)

    def mask(q):
        loads[q].wait()
        for s in range(slots):
            for b in range(q * chunk // RB, (q + 1) * chunk // RB):
                span = pl.ds(b * RB, RB)
                weight = support_ref[b, g * slots + s].astype(F32)
                cur[s, span] = held[span, s * W:(s + 1) * W] * weight

    def before(r, position):
        return position if r == 0 else plan_ref[r - 1, position]

    blocks = groups * slots
    pick, take = [], []
    for r in range(ROUNDS):
        dest = []
        for s in range(slots):
            block = before(r, g * slots + s)
            dest.append(sum(
                jnp.where(plan_ref[r, j] == block, j // slots, 0) for j in range(blocks)))
        pick.append([
            jnp.minimum(slots - 1, sum(
                jnp.where(dest[s] == lax.rem(g + o, groups), s, 0) for s in range(slots)))
            for o in range(groups)])
        take.append([])
        for s in range(slots):
            block = plan_ref[r, g * slots + s]
            take[r].append(jnp.minimum(groups - 1, sum(
                jnp.where(before(r, j) == block, j // slots, 0) for j in range(blocks))))

    pl.semaphore_wait(barrier, len(peers))

    copies, stores = [], []

    def start(copy):
        copy.start()
        copies.append(copy)
        return copy

    def dispatch(r, q):
        span = pl.ds(q * chunk, chunk)
        out = []
        for o in range(1, groups):
            send[r, o - 1, span] = cur[pick[r][o], span]
            out.append(start(pltpu.make_async_remote_copy(
                src_ref=send.at[r, o - 1, span],
                dst_ref=recv[r][q].at[g],
                send_sem=move_send.at[r, q, o - 1],
                recv_sem=move_recv.at[r, q, o - 1],
                device_id=peers[o - 1],
                device_id_type=MESH,
            )))
        recv[r][q][g] = cur[pick[r][0], span]
        return out

    def load_pair(r, k, q):
        held = recv[r][q]
        return jnp.concatenate([held[take[r][2 * k]], held[take[r][2 * k + 1]]], axis=1)

    def stage_early():
        for o in range(1, groups):
            second = pick[1][o] // 2 == 1
            left = jnp.where(second, take[0][2], take[0][0])
            right = jnp.where(second, take[0][3], take[0][1])
            early_out[o - 1, :, :W] = recv[0][0][left]
            early_out[o - 1, :, W:] = recv[0][0][right]

    def send_early():
        return [start(pltpu.make_async_remote_copy(
            src_ref=early_out.at[o - 1],
            dst_ref=early_in.at[o - 1],
            send_sem=early_send.at[o - 1],
            recv_sem=early_recv.at[o - 1],
            device_id=peers[o - 1],
            device_id_type=MESH,
        )) for o in range(1, groups)]

    share = size // members
    mine = pl.ds(pl.multiple_of(m * share, share), share)

    def send_turns():
        out = []
        for o in range(1, groups):
            wide = rot_pair[pick[1][o] // 2, mine]
            turn_out[o - 1] = jnp.where(lax.rem(pick[1][o], 2) == 0, wide[:, :W], wide[:, W:])
            out.append(start(pltpu.make_async_remote_copy(
                src_ref=turn_out.at[o - 1],
                dst_ref=turns.at[o - 1, mine],
                send_sem=turn_send.at[o - 1],
                recv_sem=turn_recv.at[o - 1],
                device_id=peers[o - 1],
                device_id_type=MESH,
            )))
        return out

    def finish_early(turned, early):
        for copy in turned:
            copy.wait_recv()
        for b in range(stages + 1):
            span = pl.ds(pl.multiple_of((m // (1 << b)) * (1 << b) * share, share), share << b)
            start(pltpu.make_async_remote_copy(
                src_ref=turns.at[:, span],
                dst_ref=turns.at[:, span],
                send_sem=spread_send.at[b],
                recv_sem=spread_recv.at[b],
                device_id=peers[groups - 1 + b],
                device_id_type=MESH,
            )).wait_recv()
        for o in range(1, groups):
            early[o - 1].wait_recv()
            source = lax.rem(g + groups - o, groups)
            recv[1][0][source] = dot3(early_in[o - 1], turns[o - 1])

    moves = []
    for q in range(CHUNKS):
        mask(q)
        moves.append(dispatch(0, q))
    for r in range(ROUNDS):
        for q in range(CHUNKS):
            for copy in moves[q]:
                copy.wait_recv()
            if r == 0 and q == CHUNKS - 1:
                early = send_early()
            for k in range(2):
                high, low = split(load_pair(r, k, q))
                mixed = dot_t(high, low)
                part = dot_t(high, high) + (mixed + mixed.T)
                acc[k] = part if q == 0 else acc[k] + part
            if r == 0 and q == 0:
                stage_early()
        for k in range(2):
            cross, tile, diagonal = pack(acc[k])
            gram_in[r, k, :W] = cross
            gram_in[r, k, W:size] = tile
            gram_in[r, k, size:] = diagonal
        swap = start(pltpu.make_async_remote_copy(
            src_ref=gram_in.at[r, 1 - core],
            dst_ref=gram_in.at[r, 2],
            send_sem=swap_send.at[r],
            recv_sem=swap_recv.at[r],
            device_id=peers[groups - 1],
            device_id_type=MESH,
        ))
        swap.wait_recv()
        total = gram_in[r, core] + gram_in[r, 2]
        for stage in range(stages):
            gram[r, 2 * stage] = total
            pair = []
            for h in range(2):
                bit = (stage + h * (stages // 2)) % stages
                part = pl.ds(0, W) if h == 0 else pl.ds(W, W + 8)
                pair.append(start(pltpu.make_async_remote_copy(
                    src_ref=gram.at[r, 2 * stage, part],
                    dst_ref=gram.at[r, 2 * stage + 1, part],
                    send_sem=sum_send.at[r, stage, h],
                    recv_sem=sum_recv.at[r, stage, h],
                    device_id=peers[groups + bit],
                    device_id_type=MESH,
                )))
            for copy in pair:
                copy.wait_recv()
            total = total + gram[r, 2 * stage + 1]
        rot[r, 0] = rotation(unpack(total), eye, stack)
        back = start(pltpu.make_async_remote_copy(
            src_ref=rot.at[r, 0],
            dst_ref=rot.at[r, 1],
            send_sem=rot_send.at[r],
            recv_sem=rot_recv.at[r],
            device_id=peers[groups - 1],
            device_id_type=MESH,
        ))
        back.wait_recv()
        rot_pair[core] = rot[r, 0]
        rot_pair[1 - core] = rot[r, 1]
        moves = []
        if r < ROUNDS - 1:
            turned_copies = send_turns()
        for q in (range(CHUNKS) if r == ROUNDS - 1 else [*range(1, CHUNKS), 0]):
            span = pl.ds(q * chunk, chunk)
            for k in range(2):
                turned = dot3(load_pair(r, k, q), rot_pair[k])
                if r == ROUNDS - 1:
                    held[span, k * size:(k + 1) * size] = turned
                else:
                    cur[2 * k, span] = turned[:, :W]
                    cur[2 * k + 1, span] = turned[:, W:]
            if r == ROUNDS - 1:
                stores.append(pltpu.make_async_copy(held.at[span], out_ref.at[span], load_sem.at[q]))
                stores[q].start()
            elif q > 0:
                moves.append(dispatch(r + 1, q))
            else:
                recv[1][0][g] = cur[pick[1][0], span]
                finish_early(turned_copies, early)
                moves.insert(0, [])
    for copy in copies:
        copy.wait_send()
    for copy in stores:
        copy.wait()


def on_device(groups, members, factor, support, plan):
    rows = factor.shape[0]
    slots = factor.shape[1] // W
    chips = members // 2
    stages = chips.bit_length() - 1
    assert slots == 4 and chips == 1 << stages and stages >= 1 and ROUNDS == 2
    size = 2 * W
    dma = pltpu.SemaphoreType.DMA
    smem = pl.BlockSpec(memory_space=pltpu.SMEM)
    return pl.pallas_call(
        functools.partial(kernel, groups, members),
        out_shape=jax.ShapeDtypeStruct(factor.shape, F32),
        in_specs=[pl.BlockSpec(memory_space=pl.ANY), smem, smem],
        out_specs=pl.BlockSpec(memory_space=pl.ANY),
        scratch_shapes=[
            pltpu.VMEM(factor.shape, F32),
            pltpu.VMEM((slots, rows, W), F32),
            pltpu.VMEM((ROUNDS, groups - 1, rows, W), F32),
            [[pltpu.VMEM((groups, rows // CHUNKS, W), F32)] * CHUNKS] * ROUNDS,
            pltpu.VMEM((groups - 1, rows // CHUNKS, size), F32),
            pltpu.VMEM((groups - 1, rows // CHUNKS, size), F32),
            pltpu.VMEM((groups - 1, size // members, W), F32),
            pltpu.VMEM((groups - 1, size, W), F32),
            pltpu.VMEM((2, size, size), F32),
            pltpu.VMEM((ROUNDS, 2 * stages, size + 8, W), F32),
            pltpu.VMEM((ROUNDS, 3, size + 8, W), F32),
            pltpu.VMEM((ROUNDS, 2, size, size), F32),
            pltpu.VMEM((2, size, size), F32),
            pltpu.VMEM((2 * size, size), F32),
            dma((CHUNKS,)),
            dma((ROUNDS, CHUNKS, groups - 1)),
            dma((ROUNDS, CHUNKS, groups - 1)),
            dma((groups - 1,)),
            dma((groups - 1,)),
            dma((groups - 1,)),
            dma((groups - 1,)),
            dma((stages + 1,)),
            dma((stages + 1,)),
            dma((ROUNDS,)),
            dma((ROUNDS,)),
            dma((ROUNDS, stages, 2)),
            dma((ROUNDS, stages, 2)),
            dma((ROUNDS,)),
            dma((ROUNDS,)),
        ],
        compiler_params=pltpu.CompilerParams(
            collective_id=0, has_side_effects=True, vmem_limit_bytes=123 * 512 * 1024
        ),
    )(factor, support.T, plan)


def solution(mesh):
    return jax.shard_map(
        functools.partial(on_device, mesh.shape["col"], mesh.shape["row"]),
        mesh=mesh,
        in_specs=(P("row", "col"), P(None, "row"), P()),
        out_specs=P("row", "col"),
        check_vma=False,
    )
```

```python
import functools

import jax
import jax.numpy as jnp
from jax import lax
from jax.experimental import pallas as pl
from jax.experimental.pallas import tpu as pltpu
from jax.sharding import PartitionSpec as P

W = 128
RB = 128
ROUNDS = 2
CHUNKS = 4
SCALED_STEPS = 7
TRUE_STEPS = 2
DAMPING = 0.01
F32 = jnp.float32
BF16 = jnp.bfloat16
MESH = pl.DeviceIdType.MESH


def split(x):
    high = x.astype(BF16)
    return high, (x - high.astype(F32)).astype(BF16)


def dot(a, b):
    return jnp.dot(a, b, preferred_element_type=F32)


def dot3(a, b):
    a_high, a_low = split(a)
    b_high, b_low = split(b)
    return dot(a_high, b_high) + (dot(a_high, b_low) + dot(a_low, b_high))


def dot_t(a, b):
    return lax.dot_general(a, b, (((0,), (0,)), ((), ())), preferred_element_type=F32)


def rotation(gram, eye, stack):
    size = gram.shape[0]
    on_diagonal = gram * eye
    diag_rows = jnp.sum(on_diagonal, axis=1, keepdims=True)
    diag_cols = jnp.sum(on_diagonal, axis=0, keepdims=True)
    spread = diag_rows - diag_cols
    joined = diag_rows + diag_cols
    half = 0.5 * gram * spread / (spread * spread + gram * gram + DAMPING * joined * joined)
    squared = dot3(half, half)
    total = jnp.sum(jnp.sum(squared * squared, axis=1, keepdims=True), axis=0, keepdims=True)
    upper = 1.0 + 1.001 * jnp.sqrt(0.5 * total)
    stack[:size] = eye - squared
    stack[size:] = eye - half

    def scaled(_, bounds):
        low, high = bounds
        scale = 2.0 / (low + high)
        delta = (high - low) / (high + low)
        factor = (2.0 * scale) * eye - (scale * scale) * stack[:size]
        stack[...] = dot3(stack[...], factor)
        return 1.0 - delta * delta, jnp.ones_like(high)

    lax.fori_loop(0, SCALED_STEPS, scaled, (jnp.ones_like(upper), upper))

    def true(_, carry):
        inverse = stack[size:]
        residual = (eye - inverse) - dot3(half, inverse)
        stack[size:] = inverse + dot3(inverse, residual)
        return carry

    lax.fori_loop(0, TRUE_STEPS, true, 0)
    return 2.0 * stack[size:] - eye


def pack(gram):
    first, last = gram[:W, :W], gram[W:, W:]
    row_ids = lax.broadcasted_iota(jnp.int32, (W, W), 0)
    col_ids = lax.broadcasted_iota(jnp.int32, (W, W), 1)
    tile = jnp.where(row_ids >= col_ids, first, last)
    diagonal = jnp.sum(jnp.where(row_ids == col_ids, last, 0.0), axis=0, keepdims=True)
    return gram[:W, W:], tile, jnp.broadcast_to(diagonal, (8, W))


def unpack(packed):
    cross, tile, diagonal = packed[:W], packed[W:2 * W], packed[2 * W:2 * W + 1]
    row_ids = lax.broadcasted_iota(jnp.int32, (W, W), 0)
    col_ids = lax.broadcasted_iota(jnp.int32, (W, W), 1)
    lower = jnp.where(row_ids > col_ids, tile, 0.0)
    upper = jnp.where(row_ids < col_ids, tile, 0.0)
    first = lower + lower.T + jnp.where(row_ids == col_ids, tile, 0.0)
    last = upper + upper.T + jnp.where(row_ids == col_ids, diagonal, 0.0)
    top = jnp.concatenate([first, cross], axis=1)
    return jnp.concatenate([top, jnp.concatenate([cross.T, last], axis=1)], axis=0)


def kernel(
    groups, members, factor_ref, support_ref, plan_ref, out_ref, rot_out,
    held, cur, send, recv, early_out, early_in, turn_out, turns,
    acc, gram, gram_in, rot, rot_pair, stack,
    load_sem, move_send, move_recv, early_send, early_recv, turn_send, turn_recv, spread_send, spread_recv,
    swap_send, swap_recv, sum_send, sum_recv, rot_send, rot_recv,
):
    slots, rows, _ = cur.shape
    size = 2 * W
    chunk = rows // CHUNKS
    chips = members // 2
    stages = chips.bit_length() - 1
    g = lax.axis_index("col")
    m = lax.axis_index("row")
    core = lax.rem(m, 2)
    chip = m // 2
    partner = m + 1 - 2 * core

    def flipped(bit):
        step = 1 << bit
        on = lax.rem(chip // step, 2)
        return (chip + step - 2 * step * on) * 2 + core

    loads = []
    for q in range(CHUNKS):
        span = pl.ds(q * chunk, chunk)
        loads.append(pltpu.make_async_copy(factor_ref.at[span], held.at[span], load_sem.at[q]))
        loads[q].start()

    peers = [{"col": lax.rem(g + o, groups), "row": m} for o in range(1, groups)]
    peers += [{"col": g, "row": partner}]
    peers += [{"col": g, "row": flipped(b)} for b in range(stages)]
    barrier = pltpu.get_barrier_semaphore()
    for peer in peers:
        pl.semaphore_signal(barrier, inc=1, device_id=peer, device_id_type=MESH)

    row_ids = lax.broadcasted_iota(jnp.int32, (size, size), 0)
    col_ids = lax.broadcasted_iota(jnp.int32, (size, size), 1)
    eye = (row_ids == col_ids).astype(F32)

    def mask(q):
        loads[q].wait()
        for s in range(slots):
            for b in range(q * chunk // RB, (q + 1) * chunk // RB):
                span = pl.ds(b * RB, RB)
                weight = support_ref[b, g * slots + s].astype(F32)
                cur[s, span] = held[span, s * W:(s + 1) * W] * weight

    def before(r, position):
        return position if r == 0 else plan_ref[r - 1, position]

    blocks = groups * slots
    pick, take = [], []
    for r in range(ROUNDS):
        dest = []
        for s in range(slots):
            block = before(r, g * slots + s)
            dest.append(sum(
                jnp.where(plan_ref[r, j] == block, j // slots, 0) for j in range(blocks)))
        pick.append([
            jnp.minimum(slots - 1, sum(
                jnp.where(dest[s] == lax.rem(g + o, groups), s, 0) for s in range(slots)))
            for o in range(groups)])
        take.append([])
        for s in range(slots):
            block = plan_ref[r, g * slots + s]
            take[r].append(jnp.minimum(groups - 1, sum(
                jnp.where(before(r, j) == block, j // slots, 0) for j in range(blocks))))

    pl.semaphore_wait(barrier, len(peers))

    copies, stores = [], []

    def start(copy):
        copy.start()
        copies.append(copy)
        return copy

    def dispatch(r, q):
        span = pl.ds(q * chunk, chunk)
        out = []
        for o in range(1, groups):
            send[r, o - 1, span] = cur[pick[r][o], span]
            out.append(start(pltpu.make_async_remote_copy(
                src_ref=send.at[r, o - 1, span],
                dst_ref=recv[r][q].at[g],
                send_sem=move_send.at[r, q, o - 1],
                recv_sem=move_recv.at[r, q, o - 1],
                device_id=peers[o - 1],
                device_id_type=MESH,
            )))
        recv[r][q][g] = cur[pick[r][0], span]
        return out

    def load_pair(r, k, q):
        held = recv[r][q]
        return jnp.concatenate([held[take[r][2 * k]], held[take[r][2 * k + 1]]], axis=1)

    def stage_early():
        for o in range(1, groups):
            second = pick[1][o] // 2 == 1
            left = jnp.where(second, take[0][2], take[0][0])
            right = jnp.where(second, take[0][3], take[0][1])
            early_out[o - 1, :, :W] = recv[0][0][left]
            early_out[o - 1, :, W:] = recv[0][0][right]

    def send_early():
        return [start(pltpu.make_async_remote_copy(
            src_ref=early_out.at[o - 1],
            dst_ref=early_in.at[o - 1],
            send_sem=early_send.at[o - 1],
            recv_sem=early_recv.at[o - 1],
            device_id=peers[o - 1],
            device_id_type=MESH,
        )) for o in range(1, groups)]

    share = size // members
    mine = pl.ds(pl.multiple_of(m * share, share), share)

    def send_turns():
        out = []
        for o in range(1, groups):
            wide = rot_pair[pick[1][o] // 2, mine]
            turn_out[o - 1] = jnp.where(lax.rem(pick[1][o], 2) == 0, wide[:, :W], wide[:, W:])
            out.append(start(pltpu.make_async_remote_copy(
                src_ref=turn_out.at[o - 1],
                dst_ref=turns.at[o - 1, mine],
                send_sem=turn_send.at[o - 1],
                recv_sem=turn_recv.at[o - 1],
                device_id=peers[o - 1],
                device_id_type=MESH,
            )))
        return out

    def finish_early(turned, early):
        for copy in turned:
            copy.wait_recv()
        for b in range(stages + 1):
            span = pl.ds(pl.multiple_of((m // (1 << b)) * (1 << b) * share, share), share << b)
            start(pltpu.make_async_remote_copy(
                src_ref=turns.at[:, span],
                dst_ref=turns.at[:, span],
                send_sem=spread_send.at[b],
                recv_sem=spread_recv.at[b],
                device_id=peers[groups - 1 + b],
                device_id_type=MESH,
            )).wait_recv()
        for o in range(1, groups):
            early[o - 1].wait_recv()
            source = lax.rem(g + groups - o, groups)
            recv[1][0][source] = dot3(early_in[o - 1], turns[o - 1])

    moves = []
    for q in range(CHUNKS):
        mask(q)
        moves.append(dispatch(0, q))
    for r in range(ROUNDS):
        for q in range(CHUNKS):
            for copy in moves[q]:
                copy.wait_recv()
            if r == 0 and q == CHUNKS - 1:
                early = send_early()
            for k in range(2):
                pair = load_pair(r, k, q)
                if r == ROUNDS - 1:
                    held[pl.ds(q * chunk, chunk), k * size:(k + 1) * size] = pair
                high, low = split(pair)
                mixed = dot_t(high, low)
                part = dot_t(high, high) + (mixed + mixed.T)
                acc[k] = part if q == 0 else acc[k] + part
            if r == 0 and q == 0:
                stage_early()
            if r == ROUNDS - 1:
                span = pl.ds(q * chunk, chunk)
                stores.append(pltpu.make_async_copy(held.at[span], out_ref.at[span], load_sem.at[q]))
                stores[q].start()
        for k in range(2):
            cross, tile, diagonal = pack(acc[k])
            gram_in[r, k, :W] = cross
            gram_in[r, k, W:size] = tile
            gram_in[r, k, size:] = diagonal
        swap = start(pltpu.make_async_remote_copy(
            src_ref=gram_in.at[r, 1 - core],
            dst_ref=gram_in.at[r, 2],
            send_sem=swap_send.at[r],
            recv_sem=swap_recv.at[r],
            device_id=peers[groups - 1],
            device_id_type=MESH,
        ))
        swap.wait_recv()
        total = gram_in[r, core] + gram_in[r, 2]
        for stage in range(stages):
            gram[r, 2 * stage] = total
            pair = []
            for h in range(2):
                bit = (stage + h * (stages // 2)) % stages
                part = pl.ds(0, W) if h == 0 else pl.ds(W, W + 8)
                pair.append(start(pltpu.make_async_remote_copy(
                    src_ref=gram.at[r, 2 * stage, part],
                    dst_ref=gram.at[r, 2 * stage + 1, part],
                    send_sem=sum_send.at[r, stage, h],
                    recv_sem=sum_recv.at[r, stage, h],
                    device_id=peers[groups + bit],
                    device_id_type=MESH,
                )))
            for copy in pair:
                copy.wait_recv()
            total = total + gram[r, 2 * stage + 1]
        rot[r, 0] = rotation(unpack(total), eye, stack)
        back = start(pltpu.make_async_remote_copy(
            src_ref=rot.at[r, 0],
            dst_ref=rot.at[r, 1],
            send_sem=rot_send.at[r],
            recv_sem=rot_recv.at[r],
            device_id=peers[groups - 1],
            device_id_type=MESH,
        ))
        back.wait_recv()
        if r == ROUNDS - 1:
            rot_out[core] = rot[r, 0]
            rot_out[1 - core] = rot[r, 1]
            break
        rot_pair[core] = rot[r, 0]
        rot_pair[1 - core] = rot[r, 1]
        moves = []
        turned_copies = send_turns()
        for q in [*range(1, CHUNKS), 0]:
            span = pl.ds(q * chunk, chunk)
            for k in range(2):
                turned = dot3(load_pair(r, k, q), rot_pair[k])
                cur[2 * k, span] = turned[:, :W]
                cur[2 * k + 1, span] = turned[:, W:]
            if q > 0:
                moves.append(dispatch(r + 1, q))
            else:
                recv[1][0][g] = cur[pick[1][0], span]
                finish_early(turned_copies, early)
                moves.insert(0, [])
    for copy in copies:
        copy.wait_send()
    for copy in stores:
        copy.wait()


def rotate_rows(rows_ref, rot_ref, out_ref):
    size = rot_ref.shape[1]
    for k in range(2):
        span = slice(k * size, (k + 1) * size)
        out_ref[:, span] = dot3(rows_ref[:, span], rot_ref[k])


def on_device(groups, members, factor, support, plan):
    rows = factor.shape[0]
    slots = factor.shape[1] // W
    chips = members // 2
    stages = chips.bit_length() - 1
    assert slots == 4 and chips == 1 << stages and stages >= 1 and ROUNDS == 2
    size = 2 * W
    dma = pltpu.SemaphoreType.DMA
    smem = pl.BlockSpec(memory_space=pltpu.SMEM)
    paired, turns = pl.pallas_call(
        functools.partial(kernel, groups, members),
        out_shape=(jax.ShapeDtypeStruct(factor.shape, F32), jax.ShapeDtypeStruct((2, size, size), F32)),
        in_specs=[pl.BlockSpec(memory_space=pl.ANY), smem, smem],
        out_specs=(pl.BlockSpec(memory_space=pl.ANY), pl.BlockSpec(memory_space=pltpu.VMEM)),
        scratch_shapes=[
            pltpu.VMEM(factor.shape, F32),
            pltpu.VMEM((slots, rows, W), F32),
            pltpu.VMEM((ROUNDS, groups - 1, rows, W), F32),
            [[pltpu.VMEM((groups, rows // CHUNKS, W), F32)] * CHUNKS] * ROUNDS,
            pltpu.VMEM((groups - 1, rows // CHUNKS, size), F32),
            pltpu.VMEM((groups - 1, rows // CHUNKS, size), F32),
            pltpu.VMEM((groups - 1, size // members, W), F32),
            pltpu.VMEM((groups - 1, size, W), F32),
            pltpu.VMEM((2, size, size), F32),
            pltpu.VMEM((ROUNDS, 2 * stages, size + 8, W), F32),
            pltpu.VMEM((ROUNDS, 3, size + 8, W), F32),
            pltpu.VMEM((ROUNDS, 2, size, size), F32),
            pltpu.VMEM((2, size, size), F32),
            pltpu.VMEM((2 * size, size), F32),
            dma((CHUNKS,)),
            dma((ROUNDS, CHUNKS, groups - 1)),
            dma((ROUNDS, CHUNKS, groups - 1)),
            dma((groups - 1,)),
            dma((groups - 1,)),
            dma((groups - 1,)),
            dma((groups - 1,)),
            dma((stages + 1,)),
            dma((stages + 1,)),
            dma((ROUNDS,)),
            dma((ROUNDS,)),
            dma((ROUNDS, stages, 2)),
            dma((ROUNDS, stages, 2)),
            dma((ROUNDS,)),
            dma((ROUNDS,)),
        ],
        compiler_params=pltpu.CompilerParams(
            collective_id=0, has_side_effects=True, vmem_limit_bytes=123 * 512 * 1024
        ),
    )(factor, support.T, plan)
    block = pl.BlockSpec((rows // 4, factor.shape[1]), lambda i: (i, 0))
    return pl.pallas_call(
        rotate_rows,
        grid=(4,),
        out_shape=jax.ShapeDtypeStruct(factor.shape, F32),
        in_specs=[block, pl.BlockSpec((2, size, size), lambda i: (0, 0, 0))],
        out_specs=block,
        compiler_params=pltpu.CompilerParams(vmem_limit_bytes=123 * 512 * 1024),
    )(paired, turns)


def solution(mesh):
    return jax.shard_map(
        functools.partial(on_device, mesh.shape["col"], mesh.shape["row"]),
        mesh=mesh,
        in_specs=(P("row", "col"), P(None, "row"), P()),
        out_specs=P("row", "col"),
        check_vma=False,
    )
```
